256 devices in a mesh: row: 8 (over y, core), col: 32 (over z, x).
Axes of the slice: x: 4, y: 4, z: 8, core: 2. Of those that a mesh axis runs over, the one named last changes fastest.
Arguments:
- upper_vectors: float32 [16384, 16384], P('row', 'col'), may hold values from -6 to 6
- lower_vectors: float32 [16384, 16384], P('row', 'col'), may hold values from -6 to 6
- secular_roots: float32 [512], replicated, may hold values from 0 to 512
- pole_values: float32 [2, 16384], P(None, ('col', 'row')), may hold values from -1 to 512, as said below
- pole_weights: float32 [2, 16384], P(None, ('col', 'row')), may hold values from -3 to 3, as said below
- undeflated: int32 [2, 16384], P(None, ('col', 'row')), may hold values from 0 to 1
Outputs:
- merged_vectors: float32 [16384, 2, 512], P(('row', 'col'))
The draws below stay inside these ranges and needn't reach their ends.
Inputs may be any that keep to these rules, and one draw needn't show every extreme that they name: `pole_values`: every pole differs from every root by 0.15 or more. `pole_weights`: magnitudes are 0.3 or more.
All inputs are finite; a program needn't handle non-finite values.
Results may differ from the reference program's by a relative error of at most 0.0003.
Values sent between devices are 32-bit elements; how exact they have to be, the bound alone decides.
No kernel may reach another device: no remote copies, remote signals or barrier semaphores. Data moves between devices by JAX's collectives and lax.ppermute only.
A program may use at most 64 MiB of HBM per device.

```python
import jax
import jax.numpy as jnp
from jax import lax

HALF = 16384
BLOCK = 512
N_ROW = 8
N_COL = 32


def draw_secular_roots(key, part):
    key = jax.random.fold_in(key, 11)
    offset = jax.random.uniform(key, (BLOCK,), jnp.float32, -0.1, 0.1)
    return jnp.arange(BLOCK).astype(jnp.float32) + 0.5 + offset


def draw_pole_values(key, part):
    key = jax.random.fold_in(key, 23)
    first, second = jax.random.split(key, 2)
    orders = jax.vmap(lambda half_key: jax.random.permutation(half_key, BLOCK))(jax.random.split(first, 2))
    position = jnp.arange(HALF) % BLOCK
    cells = orders[:, position].astype(jnp.float32)
    offset = jax.random.uniform(second, (2, HALF), jnp.float32, -0.25, 0.25)
    return cells + offset


def draw_pole_weights(key, part):
    key = jax.random.fold_in(key, 37)
    first, second = jax.random.split(key)
    side = (2 * jax.random.randint(first, (2, HALF), 0, 2) - 1).astype(jnp.float32)
    magnitude = jax.random.uniform(second, (2, HALF), jnp.float32, 0.3, 1.0)
    rising = 1.0 + 2.0 * jnp.arange(HALF).astype(jnp.float32) / (HALF - 1)
    return side * magnitude * rising[None, :]


def draw_undeflated(key, part):
    key = jax.random.fold_in(key, 41)
    first, second = jax.random.split(key)
    groups = N_COL * N_ROW
    levels = jax.random.randint(first, (2, groups, 1), 25, 96)
    values = jax.random.randint(second, (2, groups, HALF // groups), 0, 100)
    return (values < levels).astype(jnp.int32).reshape(2, HALF)


def shard_levels(own_key, extent, shards, smallest, high):
    level, own = 1.0, jax.random.fold_in(own_key, 6)
    for dim, blocks in shards:
        steps = jnp.exp(jax.random.uniform(jax.random.fold_in(own, dim), (blocks,), jnp.float32, smallest / len(shards), high / len(shards)))
        level = level * jnp.repeat(steps, extent[dim] // blocks).reshape([-1 if axis == dim else 1 for axis in range(len(extent))])
    return level


def bell_draw(key, dims, spread, most, shards=(), held_as=jnp.bfloat16):
    gain = shard_levels(key, dims, shards, -0.22, 0.18) if shards else 1.0
    array = jax.random.normal(key, dims, jnp.float32) * spread * gain
    return jnp.minimum(jnp.maximum(array, -most), most).astype(held_as)


def setup_inputs(seed: int = 0) -> dict:
    seeds = jax.random.split(jax.random.key(seed), 7)
    return {
        "upper_vectors": bell_draw(seeds[0], (HALF, HALF), 1.0, 6.0, ((0, 8), (1, 32)), jnp.float32),
        "lower_vectors": bell_draw(seeds[1], (HALF, HALF), 1.0, 6.0, ((0, 8), (1, 32)), jnp.float32),
        "secular_roots": draw_secular_roots(jax.random.fold_in(seeds[6], 71), 0),
        "pole_values": draw_pole_values(jax.random.fold_in(seeds[6], 71), 0),
        "pole_weights": draw_pole_weights(jax.random.fold_in(seeds[6], 71), 0),
        "undeflated": draw_undeflated(jax.random.fold_in(seeds[6], 71), 0),
    }


def reference(upper_vectors, lower_vectors, secular_roots, pole_values, pole_weights, undeflated):
    scaled = pole_weights * undeflated.astype(jnp.float32)
    coefficient = scaled[:, :, None] / (pole_values[:, :, None] - secular_roots[None, None, :])
    column_norm = jnp.sqrt(lax.optimization_barrier(jnp.sum(coefficient * coefficient, axis=(0, 1))))
    upper = jnp.dot(upper_vectors, coefficient[0], precision=lax.Precision.HIGHEST, preferred_element_type=jnp.float32)
    lower = jnp.dot(lower_vectors, coefficient[1], precision=lax.Precision.HIGHEST, preferred_element_type=jnp.float32)
    return jnp.stack([upper, lower], axis=1) / column_norm
```

```python
import functools

import jax
import jax.numpy as jnp
from jax import lax
from jax.experimental import pallas as pl
from jax.experimental.pallas import tpu as pltpu
from jax.sharding import PartitionSpec as P

F32 = jnp.float32
BF16 = jnp.bfloat16
ROWS = 64
WIDE = 512
HBM = pl.BlockSpec(memory_space=pltpu.HBM)
VMEM = pl.BlockSpec(memory_space=pltpu.VMEM)
KERNEL = pltpu.CompilerParams(vmem_limit_bytes=24 << 20)


def pair_e(x):
    return x ^ 1


def pair_f(x):
    return (((x + 1) ^ 1) + 3) & 3


def pair_a(z):
    return z ^ 1


def pair_b(z):
    return (((z + 1) ^ 1) + 7) & 7


def pair_c(z):
    return (11 + 4 * (((z + 1) >> 1) & 1) - z) & 7


def pair_d(z):
    return (13 - 4 * ((z >> 1) & 1) - z) & 7


X_PAIRS = ((pair_e, pair_f), (pair_f, pair_e))
Z_PAIRS = ((pair_a, pair_b, pair_c), (pair_b, pair_a, pair_d))


def partners(stream, phase):
    (e, f), (a, b, c) = X_PAIRS[stream], Z_PAIRS[stream]
    steps = (
        (("x", e), ("x", f), ("z", a), ("z", b), ("z", c)),
        (("z", a), ("z", b), ("x", e), ("x", f), ("z", c)),
    )
    pairs = []
    for row in range(8):
        for col in range(32):
            axis, pair = steps[row % 2][phase]
            z, x = divmod(col, 4)
            to = z * 4 + pair(x) if axis == "x" else pair(z) * 4 + x
            pairs.append((row * 32 + col, row * 32 + to))
    return pairs


PARTNERS = tuple(tuple(partners(stream, phase) for phase in range(5)) for stream in range(2))


def exchange(block, stream, phase):
    return lax.ppermute(block, ("row", "col"), PARTNERS[stream][phase])


def chunk_order(stream, count, first):
    core = lax.axis_index("row") & 1
    col = lax.axis_index("col")
    z, x = col >> 2, col & 3
    (e, f), (a, b, c) = X_PAIRS[stream], Z_PAIRS[stream]

    def walk(start, pairs, bits):
        for pair, bit in zip(pairs, bits):
            start = pair(start) if bit else start
        return start

    xs = {(i, j): walk(x, (e, f), (i, j)) for i in (0, 1) for j in (0, 1)}
    zs = {
        (i, j, k): walk(z, (a, b, c), (i, j, k)) for i in (0, 1) for j in (0, 1) for k in (0, 1)
    }
    order = []
    for k in range(first, first + count):
        b4, b3, b2, b1, b0 = [(k >> s) & 1 for s in (4, 3, 2, 1, 0)]
        on0 = zs[b2, b1, b0] * 4 + xs[b4, b3]
        on1 = zs[b4, b3, b0] * 4 + xs[b2, b1]
        order.append(jnp.where(core == 0, on0, on1))
    return order


def pick_kernel(stream, first, vectors, out, sems):
    copies = []
    for k, chunk in enumerate(chunk_order(stream, 16, first)):
        copies.append(
            pltpu.make_async_copy(
                vectors.at[pl.ds(pl.multiple_of(chunk * ROWS, ROWS), ROWS), :],
                out.at[pl.ds(k * ROWS, ROWS), :],
                sems.at[k],
            )
        )
    for copy in copies:
        copy.start()
    for copy in copies:
        copy.wait()


def pick(vectors, stream, first):
    return pl.pallas_call(
        functools.partial(pick_kernel, stream, first),
        out_shape=jax.ShapeDtypeStruct((16 * ROWS, WIDE), F32),
        in_specs=[HBM],
        out_specs=VMEM,
        scratch_shapes=[pltpu.SemaphoreType.DMA((16,))],
        compiler_params=KERNEL,
        cost_estimate=pl.CostEstimate(flops=0, bytes_accessed=4 << 20, transcendentals=0),
        name=("pick_upper", "pick_lower")[stream] + ("_send" if first else "_keep"),
    )(vectors)


def pack_kernel(poles, weights, undeflated, out):
    out[...] = jnp.zeros_like(out)
    out[0:2, 0:64] = poles[...]
    out[2:4, 0:64] = weights[...] * undeflated[...].astype(F32)


def pack(*arrays):
    return pl.pallas_call(
        pack_kernel,
        out_shape=jax.ShapeDtypeStruct((8, 128), F32),
        in_specs=[VMEM] * 3,
        out_specs=VMEM,
        name="pack",
    )(*arrays)


def loewner(half, root, poles, out):
    columns = poles.T
    total = jnp.zeros((8, WIDE), F32)
    for r in range(8):
        at = 8 * r + half
        value = columns[0:64, at + 2 : at + 3] / (columns[0:64, at : at + 1] - root)
        high = value.astype(BF16)
        rows = slice(r * 64, r * 64 + 64)
        out[0, rows, :] = high
        out[1, rows, :] = (value - high.astype(F32)).astype(BF16)
        total = total + jnp.sum((value * value).reshape(8, 8, WIDE), axis=0)
    return total


COEFFICIENT = jax.ShapeDtypeStruct((2, WIDE, WIDE), BF16)
SQUARES = jax.ShapeDtypeStruct((8, WIDE), F32)


def own_loewner_kernel(roots, poles, upper, lower, upper_squares, lower_squares):
    upper_squares[...] = loewner(0, roots[...], poles[...], upper)
    lower_squares[...] = loewner(1, roots[...], poles[...], lower)


def own_loewner(roots, poles):
    return pl.pallas_call(
        own_loewner_kernel,
        out_shape=[COEFFICIENT, COEFFICIENT, SQUARES, SQUARES],
        in_specs=[VMEM] * 2,
        out_specs=[VMEM] * 4,
        compiler_params=KERNEL,
        cost_estimate=pl.CostEstimate(flops=1 << 23, bytes_accessed=2 << 20, transcendentals=1 << 19),
        name="loewner",
    )(roots, poles)


def product(vectors, high, low):
    a = vectors.astype(BF16)
    rest = (vectors - a.astype(F32)).astype(BF16)
    dot = functools.partial(jnp.dot, preferred_element_type=F32)
    return dot(a, high) + (dot(a, low) + dot(rest, high))


def own_kernel(vectors, coefficient, out):
    for k in range(0, 16 * ROWS, 256):
        out[k : k + 256, :] = product(vectors[k : k + 256, :], coefficient[0], coefficient[1])


def own_products(vectors, coefficient, name):
    return pl.pallas_call(
        own_kernel,
        out_shape=jax.ShapeDtypeStruct((16 * ROWS, WIDE), F32),
        in_specs=[VMEM] * 2,
        out_specs=VMEM,
        compiler_params=KERNEL,
        cost_estimate=pl.CostEstimate(flops=3 << 30, bytes_accessed=6 << 20, transcendentals=0),
        name=name,
    )(vectors, coefficient)


def meet_kernel(stream, roots, poles, vectors, own, squares, send, coefficient, sums):
    total = squares[...] + loewner(stream, roots[...], poles[...], coefficient)
    for k in range(0, 8 * ROWS, 256):
        rows = slice(8 * ROWS + k, 8 * ROWS + k + 256)
        send[k : k + 256, :] = own[rows, :] + product(
            vectors[rows, :], coefficient[0], coefficient[1]
        )
    send[8 * ROWS :, :] = total
    sums[...] = total


def meet(stream, *arrays):
    return pl.pallas_call(
        functools.partial(meet_kernel, stream),
        out_shape=[jax.ShapeDtypeStruct((8 * ROWS + 8, WIDE), F32), COEFFICIENT, SQUARES],
        in_specs=[VMEM] * 5,
        out_specs=[VMEM] * 3,
        compiler_params=KERNEL,
        cost_estimate=pl.CostEstimate(flops=3 << 29, bytes_accessed=6 << 20, transcendentals=0),
        name=f"meet_{stream}",
    )(*arrays)


def rest_kernel(vectors, coefficient, own, out):
    for k in range(0, 8 * ROWS, 256):
        rows = slice(k, k + 256)
        out[rows, :] = own[rows, :] + product(vectors[rows, :], coefficient[0], coefficient[1])


def rest(stream, *arrays):
    return pl.pallas_call(
        rest_kernel,
        out_shape=jax.ShapeDtypeStruct((8 * ROWS, WIDE), F32),
        in_specs=[VMEM] * 3,
        out_specs=VMEM,
        compiler_params=KERNEL,
        cost_estimate=pl.CostEstimate(flops=3 << 29, bytes_accessed=6 << 20, transcendentals=0),
        name=f"rest_{stream}",
    )(*arrays)


def add_kernel(half, kept, arrived, squares, send, keep, sums):
    send[:half, :] = kept[half:, :] + arrived[half : 2 * half, :]
    total = squares[...] + arrived[2 * half :, :]
    send[half:, :] = total
    sums[...] = total
    keep[...] = kept[:half, :] + arrived[:half, :]


def add(half, kept, arrived, squares, name):
    return pl.pallas_call(
        functools.partial(add_kernel, half),
        out_shape=[
            jax.ShapeDtypeStruct((half + 8, WIDE), F32),
            jax.ShapeDtypeStruct((half, WIDE), F32),
            jax.ShapeDtypeStruct((8, WIDE), F32),
        ],
        in_specs=[VMEM] * 3,
        out_specs=[VMEM] * 3,
        compiler_params=KERNEL,
        name=name,
    )(kept, arrived, squares)


def finish_kernel(upper, lower, to_upper, to_lower, upper_squares, lower_squares, out):
    squares = upper_squares[...] + lower_squares[...] + to_upper[ROWS:, :] + to_lower[ROWS:, :]
    norm = jnp.sqrt(jnp.sum(squares, axis=0, keepdims=True))
    out[:, 0, :] = (upper[...] + to_upper[:ROWS, :]) / norm
    out[:, 1, :] = (lower[...] + to_lower[:ROWS, :]) / norm


def local(upper_vectors, lower_vectors, secular_roots, pole_values, pole_weights, undeflated):
    vectors = [pltpu.with_memory_space_constraint(v, pltpu.HBM) for v in (upper_vectors, lower_vectors)]
    roots = secular_roots.reshape(1, WIDE)
    sent = [pick(vectors[s], s, 16) for s in (0, 1)]
    packed = pack(pole_values, pole_weights, undeflated)
    *sent, packed = lax.optimization_barrier((*sent, packed))
    arrived = [exchange(sent[s], s, 0) for s in (0, 1)]
    poles = lax.all_gather(packed, "row", axis=0, tiled=True)
    met = [exchange(poles, s, 0) for s in (0, 1)]
    mine = [pick(vectors[s], s, 0) for s in (0, 1)]
    *coefficients, upper_squares, lower_squares = own_loewner(roots, poles)
    squares = [upper_squares, lower_squares]
    own = [own_products(mine[s], coefficients[s], f"own_{s}") for s in (0, 1)]
    send, keep = [None] * 2, [None] * 2
    for s in (0, 1):
        send[s], coefficients[s], squares[s] = meet(s, roots, met[s], arrived[s], own[s], squares[s])
    for s in (0, 1):
        keep[s] = rest(s, arrived[s], coefficients[s], own[s])
    for phase in (1, 2, 3):
        half = ROWS << (3 - phase)
        for s in (0, 1):
            arrived[s] = exchange(send[s], s, phase)
        for s in (0, 1):
            send[s], keep[s], squares[s] = add(half, keep[s], arrived[s], squares[s], f"add_{phase}_{s}")
    arrived = [exchange(send[s], s, 4) for s in (0, 1)]
    return pl.pallas_call(
        finish_kernel,
        out_shape=jax.ShapeDtypeStruct((ROWS, 2, WIDE), F32),
        in_specs=[VMEM] * 6,
        out_specs=VMEM,
        compiler_params=KERNEL,
        name="finish",
    )(*keep, *arrived, *squares)


def solution(mesh):
    return jax.shard_map(
        local,
        mesh=mesh,
        in_specs=(
            P("row", "col"),
            P("row", "col"),
            P(),
            P(None, ("col", "row")),
            P(None, ("col", "row")),
            P(None, ("col", "row")),
        ),
        out_specs=P(("row", "col"), None, None),
        check_vma=False,
    )
```

```python
import functools

import jax
import jax.numpy as jnp
from jax import lax
from jax.experimental import pallas as pl
from jax.experimental.pallas import tpu as pltpu
from jax.sharding import PartitionSpec as P

F32 = jnp.float32
BF16 = jnp.bfloat16
ROWS = 64
PART = 32
WIDE = 512
HBM = pl.BlockSpec(memory_space=pltpu.HBM)
VMEM = pl.BlockSpec(memory_space=pltpu.VMEM)
KERNEL = pltpu.CompilerParams(vmem_limit_bytes=16 << 20)


def pair_e(x):
    return x ^ 1


def pair_f(x):
    return (((x + 1) ^ 1) + 3) & 3


def pair_a(z):
    return z ^ 1


def pair_b(z):
    return (((z + 1) ^ 1) + 7) & 7


def pair_c(z):
    return (11 + 4 * (((z + 1) >> 1) & 1) - z) & 7


def pair_d(z):
    return (13 - 4 * ((z >> 1) & 1) - z) & 7


STEPS = (
    (
        (("z", pair_a), ("z", pair_b), ("x", pair_f), ("x", pair_e), ("z", pair_c)),
        (("z", pair_b), ("z", pair_a), ("x", pair_e), ("x", pair_f), ("z", pair_d)),
    ),
    (
        (("x", pair_e), ("x", pair_f), ("z", pair_a), ("z", pair_b), ("z", pair_c)),
        (("x", pair_f), ("x", pair_e), ("z", pair_b), ("z", pair_a), ("z", pair_d)),
    ),
)


def partners(stream, phase):
    pairs = []
    for row in range(8):
        for col in range(32):
            axis, pair = STEPS[stream][row % 2][phase]
            z, x = divmod(col, 4)
            to = z * 4 + pair(x) if axis == "x" else pair(z) * 4 + x
            pairs.append((row * 32 + col, row * 32 + to))
    return pairs


PARTNERS = tuple(tuple(partners(stream, phase) for phase in range(5)) for stream in range(2))


def exchange(block, stream, phase):
    return lax.ppermute(block, ("row", "col"), PARTNERS[stream][phase])


def chunk_order(stream, count, first):
    core = lax.axis_index("row") & 1
    col = lax.axis_index("col")
    known = {}

    def place(side, axis, bits):
        key = (side, axis, bits)
        if key not in known:
            if not bits:
                known[key] = (col >> 2) if axis == "z" else (col & 3)
            else:
                pairs = [pair for on, pair in STEPS[stream][side] if on == axis]
                before = place(side, axis, bits[:-1])
                known[key] = pairs[len(bits) - 1](before) if bits[-1] else before
        return known[key]

    order = []
    for k in range(first, first + count):
        taken = [(k >> shift) & 1 for shift in (4, 3, 2, 1, 0)]
        on = []
        for side in (0, 1):
            bits = {
                axis: tuple(bit for bit, (at, _) in zip(taken, STEPS[stream][side]) if at == axis)
                for axis in ("x", "z")
            }
            on.append(place(side, "z", bits["z"]) * 4 + place(side, "x", bits["x"]))
        order.append(jnp.where(core == 0, on[0], on[1]))
    return order


def copy_rows(stream, first, vectors, out, sems):
    order = chunk_order(stream, 16, first)
    copies = []
    for n in range(32):
        batch, k = divmod(n, 16)
        at = pl.multiple_of(order[k] * ROWS + batch * PART, PART)
        copies.append(
            pltpu.make_async_copy(
                vectors.at[pl.ds(at, PART), :], out.at[pl.ds(n * PART, PART), :], sems.at[n]
            )
        )
    return copies


def pick_upper_kernel(vectors, out, rows, sems):
    arriving = copy_rows(0, 16, vectors, rows, sems.at[0])
    for copy in arriving:
        copy.start()
    leaving = []
    for k, copy in enumerate(arriving):
        copy.wait()
        at = pl.ds(k * PART, PART)
        leaving.append(pltpu.make_async_copy(rows.at[at, :], out.at[at, :], sems.at[1, k]))
        leaving[k].start()
    for copy in leaving:
        copy.wait()


def pick_lower_kernel(vectors, out, sems):
    copies = copy_rows(1, 16, vectors, out, sems)
    for copy in copies:
        copy.start()
    for copy in copies:
        copy.wait()


def pick_upper(vectors):
    return pl.pallas_call(
        pick_upper_kernel,
        out_shape=jax.ShapeDtypeStruct((16 * ROWS, WIDE), F32),
        in_specs=[HBM],
        out_specs=HBM,
        scratch_shapes=[pltpu.VMEM((16 * ROWS, WIDE), F32), pltpu.SemaphoreType.DMA((2, 32))],
        compiler_params=pltpu.CompilerParams(vmem_limit_bytes=4 << 20),
        cost_estimate=pl.CostEstimate(flops=0, bytes_accessed=4 << 20, transcendentals=0),
        name="pick_upper",
    )(vectors)


def pick_lower(vectors):
    return pl.pallas_call(
        pick_lower_kernel,
        out_shape=jax.ShapeDtypeStruct((16 * ROWS, WIDE), F32),
        in_specs=[HBM],
        out_specs=VMEM,
        scratch_shapes=[pltpu.SemaphoreType.DMA((32,))],
        compiler_params=pltpu.CompilerParams(vmem_limit_bytes=4 << 20),
        cost_estimate=pl.CostEstimate(flops=0, bytes_accessed=4 << 20, transcendentals=0),
        name="pick_lower",
    )(vectors)


def pack_kernel(poles, weights, undeflated, out):
    out[...] = jnp.zeros_like(out)
    scaled = weights[...] * undeflated[...].astype(F32)
    for r in range(8):
        out[8 * r : 8 * r + 2, 0:64] = poles[...]
        out[8 * r + 2 : 8 * r + 4, 0:64] = scaled


def pack(*arrays):
    return pl.pallas_call(
        pack_kernel,
        out_shape=jax.ShapeDtypeStruct((64, 128), F32),
        in_specs=[VMEM] * 3,
        out_specs=VMEM,
        name="pack",
    )(*arrays)


def loewner(half, root, poles, out):
    columns = poles.T
    total = jnp.zeros((8, WIDE), F32)
    for r in range(8):
        at = 8 * r + half
        value = columns[0:64, at + 2 : at + 3] / (columns[0:64, at : at + 1] - root)
        high = value.astype(BF16)
        rows = slice(r * 64, r * 64 + 64)
        out[0, rows, :] = high
        out[1, rows, :] = (value - high.astype(F32)).astype(BF16)
        total = total + jnp.sum((value * value).reshape(8, 8, WIDE), axis=0)
    return total


COEFFICIENT = jax.ShapeDtypeStruct((2, WIDE, WIDE), BF16)
SQUARES = jax.ShapeDtypeStruct((8, WIDE), F32)


def own_loewner_kernel(roots, poles, upper, lower, upper_squares, lower_squares):
    upper_squares[...] = loewner(0, roots[...], poles[...], upper)
    lower_squares[...] = loewner(1, roots[...], poles[...], lower)


def own_loewner(roots, poles):
    return pl.pallas_call(
        own_loewner_kernel,
        out_shape=[COEFFICIENT, COEFFICIENT, SQUARES, SQUARES],
        in_specs=[VMEM] * 2,
        out_specs=[VMEM] * 4,
        compiler_params=KERNEL,
        cost_estimate=pl.CostEstimate(flops=1 << 23, bytes_accessed=2 << 20, transcendentals=1 << 19),
        name="loewner",
    )(roots, poles)


def product(vectors, high, low):
    a = vectors.astype(BF16)
    rest = (vectors - a.astype(F32)).astype(BF16)
    dot = functools.partial(jnp.dot, preferred_element_type=F32)
    return dot(a, high) + (dot(a, low) + dot(rest, high))


def own_kernel(upper, lower, upper_part, lower_part, upper_out, lower_out, rows, sems):
    streams = ((upper, upper_part, upper_out), (lower, lower_part, lower_out))
    copies = [copy_rows(s, 0, streams[s][0], rows.at[s], sems.at[s]) for s in (0, 1)]
    for copy in copies[0] + copies[1]:
        copy.start()
    for s, (_, part, out) in enumerate(streams):
        for k in range(0, 32, 8):
            for copy in copies[s][k : k + 8]:
                copy.wait()
            at = slice(k * PART, k * PART + 256)
            out[at, :] = product(rows[s, at, :], part[0], part[1])


def own_products(upper, lower, upper_part, lower_part):
    out = jax.ShapeDtypeStruct((16 * ROWS, WIDE), F32)
    return pl.pallas_call(
        own_kernel,
        out_shape=[out, out],
        in_specs=[HBM] * 2 + [VMEM] * 2,
        out_specs=[VMEM] * 2,
        scratch_shapes=[pltpu.VMEM((2, 16 * ROWS, WIDE), F32), pltpu.SemaphoreType.DMA((2, 32))],
        compiler_params=KERNEL,
        cost_estimate=pl.CostEstimate(flops=6 << 30, bytes_accessed=8 << 20, transcendentals=0),
        name="own",
    )(upper, lower, upper_part, lower_part)


def shape(rows, squares=False):
    return jax.ShapeDtypeStruct((rows + 8 if squares else rows, WIDE), F32)


def call(kernel, out_shape, *arrays, name, flops=0, from_hbm=None, scratch=()):
    return pl.pallas_call(
        kernel,
        out_shape=out_shape,
        in_specs=[HBM if n == from_hbm else VMEM for n in range(len(arrays))],
        out_specs=jax.tree.map(lambda _: VMEM, out_shape),
        scratch_shapes=scratch,
        compiler_params=KERNEL,
        cost_estimate=pl.CostEstimate(flops=flops, bytes_accessed=1 << 20, transcendentals=0),
        name=name,
    )(*arrays)


def meet_kernel(stream, vectors, own, roots, poles, squares, send, coefficient, sums, rows, sems):
    copies = []
    for n, first in enumerate((256, 768, 0, 512)):
        at = pl.ds(first, 256)
        copies.append(pltpu.make_async_copy(vectors.at[at, :], rows.at[at, :], sems.at[n]))
        copies[n].start()
    total = squares[...] + loewner(stream, roots[...], poles[...], coefficient)
    send[256:, :] = total
    sums[...] = total
    copies[0].wait()
    send[:256, :] = own[256:512, :] + product(rows[256:512, :], coefficient[0], coefficient[1])
    for copy in copies[1:]:
        copy.wait()


def meet(stream, *arrays):
    return call(
        functools.partial(meet_kernel, stream),
        [shape(256, True), COEFFICIENT, SQUARES, shape(16 * ROWS)],
        *arrays,
        name=f"meet_{stream}",
        flops=1 << 30,
        from_hbm=0,
        scratch=[pltpu.SemaphoreType.DMA((4,))],
    )


def add_own_kernel(first, vectors, own, coefficient, out):
    at = slice(first, first + 256)
    out[...] = own[at, :] + product(vectors[at, :], coefficient[0], coefficient[1])


def add_own(first, *arrays, name):
    return call(functools.partial(add_own_kernel, first), shape(256), *arrays, name=name, flops=1 << 30)


def add_kernel(half, kept, arrived, *refs):
    if len(refs) > 3:
        squares, _, send, keep, sums = refs
        total = squares[...] + arrived[2 * half :, :]
        send[half:, :] = total
        sums[...] = total
    else:
        _, send, keep = refs
    send[:half, :] = kept[half:, :] + arrived[half : 2 * half, :]
    keep[...] = kept[:half, :] + arrived[:half, :]


def add(half, kept, arrived, squares, after, name):
    kernel = functools.partial(add_kernel, half)
    if squares is None:
        return *call(kernel, [shape(half), shape(half)], kept, arrived, after, name=name), None
    return call(kernel, [shape(half, True), shape(half), SQUARES], kept, arrived, squares, after, name=name)


def join_kernel(upper, lower, upper_in, lower_in, *refs):
    if len(refs) > 4:
        upper_squares, lower_squares, send, up, low, sums = refs
        total = upper_squares[...] + lower_squares[...]
        total = total + (upper_in[2 * PART :, :] + lower_in[2 * PART :, :])
        send[2 * PART :, :] = total
        sums[...] = total
    else:
        _, send, up, low = refs
    send[:PART, :] = upper[PART:, :] + upper_in[PART : 2 * PART, :]
    send[PART : 2 * PART, :] = lower[PART:, :] + lower_in[PART : 2 * PART, :]
    up[...] = upper[:PART, :] + upper_in[:PART, :]
    low[...] = lower[:PART, :] + lower_in[:PART, :]


def join(batch, *arrays):
    out = [shape(2 * PART, batch == 0), shape(PART), shape(PART)] + [SQUARES] * (batch == 0)
    return call(join_kernel, out, *arrays, name=f"join_{batch}")


def finish_kernel(squares, arrived, upper, lower, late, late_upper, late_lower, out):
    norm = jnp.sqrt(jnp.sum(squares[...] + arrived[2 * PART :, :], axis=0, keepdims=True))
    for first, up, low, came in ((0, upper, lower, arrived), (PART, late_upper, late_lower, late)):
        out[first : first + PART, 0, :] = (up[...] + came[:PART, :]) / norm
        out[first : first + PART, 1, :] = (low[...] + came[PART : 2 * PART, :]) / norm


def local(upper_vectors, lower_vectors, secular_roots, pole_values, pole_weights, undeflated):
    vectors = [pltpu.with_memory_space_constraint(v, pltpu.HBM) for v in (upper_vectors, lower_vectors)]
    roots = secular_roots.reshape(1, WIDE)
    sent = (pick_upper(vectors[0]), pick_lower(vectors[1]))
    raw = [pltpu.with_memory_space_constraint(exchange(sent[s], s, 0), pltpu.HBM) for s in (0, 1)]
    packed = pack(pole_values, pole_weights, undeflated)
    poles = lax.all_to_all(packed, "row", split_axis=0, concat_axis=0, tiled=True)
    met = [exchange(poles, s, 0) for s in (0, 1)]
    *coefficients, upper_squares, lower_squares = own_loewner(roots, poles)
    own = own_products(*vectors, *coefficients)

    streams = [(s, batch) for batch in (0, 1) for s in (0, 1)]
    squares = {(s, 1): None for s in (0, 1)} | {(0, 0): upper_squares, (1, 0): lower_squares}
    send, keep, arrived, parts = {}, {}, {}, {}
    for s in (0, 1):
        send[s, 0], parts[s], squares[s, 0], raw[s] = meet(s, raw[s], own[s], roots, met[s], squares[s, 0])
    for s in (0, 1):
        send[s, 1] = add_own(768, raw[s], own[s], parts[s], name=f"meet_{s}_late")
    for s, batch in streams:
        keep[s, batch] = add_own(512 * batch, raw[s], own[s], parts[s], name=f"rest_{s}_{batch}")
    after = send[1, 1]
    for phase in (1, 2):
        for at in streams:
            arrived[at] = exchange(send[at], at[0], phase)
        for at in streams:
            half, name = PART << (3 - phase), "add_{}_{}_{}".format(phase, *at)
            send[at], keep[at], squares[at] = add(half, keep[at], arrived[at], squares[at], after, name)
            after = keep[at]
    for at in streams:
        arrived[at] = exchange(send[at], at[0], 3)
    early = join(0, *(group[s, 0] for group in (keep, arrived, squares) for s in (0, 1)))
    late = join(1, *(group[s, 1] for group in (keep, arrived) for s in (0, 1)), early[1])
    return call(
        finish_kernel,
        jax.ShapeDtypeStruct((ROWS, 2, WIDE), F32),
        early[3],
        exchange(early[0], 0, 4),
        *early[1:3],
        exchange(late[0], 0, 4),
        *late[1:3],
        name="finish",
    )


def solution(mesh):
    return jax.shard_map(
        local,
        mesh=mesh,
        in_specs=(
            P("row", "col"),
            P("row", "col"),
            P(),
            P(None, ("col", "row")),
            P(None, ("col", "row")),
            P(None, ("col", "row")),
        ),
        out_specs=P(("row", "col"), None, None),
        check_vma=False,
    )
```

```python
import functools

import jax
import jax.numpy as jnp
from jax import lax
from jax.experimental import pallas as pl
from jax.experimental.pallas import tpu as pltpu
from jax.sharding import PartitionSpec as P

F32 = jnp.float32
BF16 = jnp.bfloat16
ROWS = 64
PART = 32
WIDE = 512
HBM = pl.BlockSpec(memory_space=pltpu.HBM)
VMEM = pl.BlockSpec(memory_space=pltpu.VMEM)
KERNEL = pltpu.CompilerParams(vmem_limit_bytes=16 << 20)


def pair_e(x):
    return x ^ 1


def pair_f(x):
    return (((x + 1) ^ 1) + 3) & 3


def pair_a(z):
    return z ^ 1


def pair_b(z):
    return (((z + 1) ^ 1) + 7) & 7


def pair_c(z):
    return (11 + 4 * (((z + 1) >> 1) & 1) - z) & 7


def pair_d(z):
    return (13 - 4 * ((z >> 1) & 1) - z) & 7


STEPS = (
    (
        (("z", pair_a), ("z", pair_b), ("x", pair_f), ("x", pair_e), ("z", pair_c)),
        (("z", pair_b), ("z", pair_a), ("x", pair_e), ("x", pair_f), ("z", pair_d)),
    ),
    (
        (("x", pair_e), ("x", pair_f), ("z", pair_a), ("z", pair_b), ("z", pair_c)),
        (("x", pair_f), ("x", pair_e), ("z", pair_b), ("z", pair_a), ("z", pair_d)),
    ),
)


def partners(stream, phase):
    pairs = []
    for row in range(8):
        for col in range(32):
            axis, pair = STEPS[stream][row % 2][phase]
            z, x = divmod(col, 4)
            to = z * 4 + pair(x) if axis == "x" else pair(z) * 4 + x
            pairs.append((row * 32 + col, row * 32 + to))
    return pairs


CORES = [(device, device ^ 32) for device in range(256)]
PARTNERS = tuple(tuple(partners(stream, phase) for phase in range(5)) for stream in range(2))


def exchange(block, stream, phase):
    return lax.ppermute(block, ("row", "col"), PARTNERS[stream][phase])


def chunk_order(stream, count, first):
    core = lax.axis_index("row") & 1
    col = lax.axis_index("col")
    known = {}

    def place(side, axis, bits):
        key = (side, axis, bits)
        if key not in known:
            if not bits:
                known[key] = (col >> 2) if axis == "z" else (col & 3)
            else:
                pairs = [pair for on, pair in STEPS[stream][side] if on == axis]
                before = place(side, axis, bits[:-1])
                known[key] = pairs[len(bits) - 1](before) if bits[-1] else before
        return known[key]

    order = []
    for k in range(first, first + count):
        taken = [(k >> shift) & 1 for shift in (4, 3, 2, 1, 0)]
        on = []
        for side in (0, 1):
            bits = {
                axis: tuple(bit for bit, (at, _) in zip(taken, STEPS[stream][side]) if at == axis)
                for axis in ("x", "z")
            }
            on.append(place(side, "z", bits["z"]) * 4 + place(side, "x", bits["x"]))
        order.append(jnp.where(core == 0, on[0], on[1]))
    return order


def copy_rows(stream, first, vectors, out, sems):
    order = chunk_order(stream, 16, first)
    copies = []
    for n in range(32):
        batch, k = divmod(n, 16)
        at = pl.multiple_of(order[k] * ROWS + batch * PART, PART)
        copies.append(
            pltpu.make_async_copy(
                vectors.at[pl.ds(at, PART), :], out.at[pl.ds(n * PART, PART), :], sems.at[n]
            )
        )
    return copies


def pick_kernel(stream, vectors, out, rows, sems):
    arriving = copy_rows(stream, 16, vectors, rows, sems.at[0])
    for copy in arriving:
        copy.start()
    leaving = []
    for k, copy in enumerate(arriving):
        copy.wait()
        at = pl.ds(k * PART, PART)
        leaving.append(pltpu.make_async_copy(rows.at[at, :], out.at[at, :], sems.at[1, k]))
        leaving[k].start()
    for copy in leaving:
        copy.wait()


def pick(stream, vectors):
    return pl.pallas_call(
        functools.partial(pick_kernel, stream),
        out_shape=jax.ShapeDtypeStruct((16 * ROWS, WIDE), F32),
        in_specs=[HBM],
        out_specs=HBM,
        scratch_shapes=[pltpu.VMEM((16 * ROWS, WIDE), F32), pltpu.SemaphoreType.DMA((2, 32))],
        compiler_params=pltpu.CompilerParams(vmem_limit_bytes=4 << 20),
        cost_estimate=pl.CostEstimate(flops=0, bytes_accessed=4 << 20, transcendentals=0),
        name=f"pick_{stream}",
    )(vectors)


def pack_kernel(poles, weights, undeflated, out):
    out[...] = jnp.zeros_like(out)
    scaled = weights[...] * undeflated[...].astype(F32)
    for r in range(8):
        out[8 * r : 8 * r + 2, 0:64] = poles[...]
        out[8 * r + 2 : 8 * r + 4, 0:64] = scaled


def pack(*arrays):
    return pl.pallas_call(
        pack_kernel,
        out_shape=jax.ShapeDtypeStruct((64, 128), F32),
        in_specs=[VMEM] * 3,
        out_specs=VMEM,
        name="pack",
    )(*arrays)


def loewner(half, root, poles, out):
    columns = poles.T
    total = jnp.zeros((8, WIDE), F32)
    for r in range(8):
        at = 8 * r + half
        value = columns[0:64, at + 2 : at + 3] / (columns[0:64, at : at + 1] - root)
        high = value.astype(BF16)
        rows = slice(r * 64, r * 64 + 64)
        out[0, rows, :] = high
        out[1, rows, :] = (value - high.astype(F32)).astype(BF16)
        total = total + jnp.sum((value * value).reshape(8, 8, WIDE), axis=0)
    return total


COEFFICIENT = jax.ShapeDtypeStruct((2, WIDE, WIDE), BF16)
SQUARES = jax.ShapeDtypeStruct((8, WIDE), F32)


def own_loewner_kernel(roots, poles, upper, lower, upper_squares, lower_squares):
    upper_squares[...] = loewner(0, roots[...], poles[...], upper)
    lower_squares[...] = loewner(1, roots[...], poles[...], lower)


def own_loewner(roots, poles):
    return pl.pallas_call(
        own_loewner_kernel,
        out_shape=[COEFFICIENT, COEFFICIENT, SQUARES, SQUARES],
        in_specs=[VMEM] * 2,
        out_specs=[VMEM] * 4,
        compiler_params=KERNEL,
        cost_estimate=pl.CostEstimate(flops=1 << 23, bytes_accessed=2 << 20, transcendentals=1 << 19),
        name="loewner",
    )(roots, poles)


def product(vectors, high, low):
    a = vectors.astype(BF16)
    rest = (vectors - a.astype(F32)).astype(BF16)
    dot = functools.partial(jnp.dot, preferred_element_type=F32)
    return dot(a, high) + (dot(a, low) + dot(rest, high))


def own_kernel(upper, lower, upper_part, lower_part, upper_out, lower_out, rows, sems):
    streams = ((upper, upper_part, upper_out), (lower, lower_part, lower_out))
    copies = [copy_rows(s, 0, streams[s][0], rows.at[s], sems.at[s]) for s in (0, 1)]
    for copy in copies[0] + copies[1]:
        copy.start()
    for s, (_, part, out) in enumerate(streams):
        for k in range(0, 32, 8):
            for copy in copies[s][k : k + 8]:
                copy.wait()
            at = slice(k * PART, k * PART + 256)
            out[at, :] = product(rows[s, at, :], part[0], part[1])


def own_products(upper, lower, upper_part, lower_part):
    out = jax.ShapeDtypeStruct((16 * ROWS, WIDE), F32)
    return pl.pallas_call(
        own_kernel,
        out_shape=[out, out],
        in_specs=[HBM] * 2 + [VMEM] * 2,
        out_specs=[VMEM] * 2,
        scratch_shapes=[pltpu.VMEM((2, 16 * ROWS, WIDE), F32), pltpu.SemaphoreType.DMA((2, 32))],
        compiler_params=KERNEL,
        cost_estimate=pl.CostEstimate(flops=6 << 30, bytes_accessed=8 << 20, transcendentals=0),
        name="own",
    )(upper, lower, upper_part, lower_part)


def shape(rows, squares=False):
    return jax.ShapeDtypeStruct((rows + 8 if squares else rows, WIDE), F32)


def call(kernel, out_shape, *arrays, name, flops=0, from_hbm=None, scratch=()):
    return pl.pallas_call(
        kernel,
        out_shape=out_shape,
        in_specs=[HBM if n == from_hbm else VMEM for n in range(len(arrays))],
        out_specs=jax.tree.map(lambda _: VMEM, out_shape),
        scratch_shapes=scratch,
        compiler_params=KERNEL,
        cost_estimate=pl.CostEstimate(flops=flops, bytes_accessed=1 << 20, transcendentals=0),
        name=name,
    )(*arrays)


def meet_kernel(stream, vectors, own, roots, poles, squares, send, coefficient, sums, rows, sems):
    copies = []
    for n, first in enumerate((256, 768, 0, 512)):
        at = pl.ds(first, 256)
        copies.append(pltpu.make_async_copy(vectors.at[at, :], rows.at[at, :], sems.at[n]))
        copies[n].start()
    total = squares[...] + loewner(stream, roots[...], poles[...], coefficient)
    send[256:, :] = total
    sums[...] = total
    copies[0].wait()
    send[:256, :] = own[256:512, :] + product(rows[256:512, :], coefficient[0], coefficient[1])
    for copy in copies[1:]:
        copy.wait()


def meet_direct(stream, *arrays):
    return call(
        functools.partial(meet_direct_kernel, stream),
        [shape(256, True), COEFFICIENT, SQUARES],
        *arrays,
        name=f"meet_{stream}",
        flops=1 << 30,
    )


def meet(stream, *arrays):
    return call(
        functools.partial(meet_kernel, stream),
        [shape(256, True), COEFFICIENT, SQUARES, shape(16 * ROWS)],
        *arrays,
        name=f"meet_{stream}",
        flops=1 << 30,
        from_hbm=0,
        scratch=[pltpu.SemaphoreType.DMA((4,))],
    )


def meet_direct_kernel(stream, vectors, own, roots, poles, squares, send, coefficient, sums):
    total = squares[...] + loewner(stream, roots[...], poles[...], coefficient)
    send[256:, :] = total
    sums[...] = total
    send[:256, :] = own[256:512, :] + product(vectors[256:512, :], coefficient[0], coefficient[1])


def add_own_kernel(first, vectors, own, coefficient, out):
    at = slice(first, first + 256)
    out[...] = own[at, :] + product(vectors[at, :], coefficient[0], coefficient[1])


def add_own(first, *arrays, name):
    return call(functools.partial(add_own_kernel, first), shape(256), *arrays, name=name, flops=1 << 30)


def add_kernel(half, kept, arrived, *refs):
    if len(refs) > 3:
        squares, _, send, keep, sums = refs
        total = squares[...] + arrived[2 * half :, :]
        send[half:, :] = total
        sums[...] = total
    else:
        _, send, keep = refs
    send[:half, :] = kept[half:, :] + arrived[half : 2 * half, :]
    keep[...] = kept[:half, :] + arrived[:half, :]


def add(half, kept, arrived, squares, after, name):
    kernel = functools.partial(add_kernel, half)
    if squares is None:
        return *call(kernel, [shape(half), shape(half)], kept, arrived, after, name=name), None
    return call(kernel, [shape(half, True), shape(half), SQUARES], kept, arrived, squares, after, name=name)


def join_kernel(upper, lower, upper_in, lower_in, *refs):
    if len(refs) > 4:
        upper_squares, lower_squares, _, send, up, low, sums = refs
        total = upper_squares[...] + lower_squares[...]
        total = total + (upper_in[2 * PART :, :] + lower_in[2 * PART :, :])
        send[2 * PART :, :] = total
        sums[...] = total
    else:
        _, send, up, low = refs
    send[:PART, :] = upper[PART:, :] + upper_in[PART : 2 * PART, :]
    send[PART : 2 * PART, :] = lower[PART:, :] + lower_in[PART : 2 * PART, :]
    up[...] = upper[:PART, :] + upper_in[:PART, :]
    low[...] = lower[:PART, :] + lower_in[:PART, :]


def join(batch, *arrays):
    out = [shape(2 * PART, batch == 0), shape(PART), shape(PART)] + [SQUARES] * (batch == 0)
    return call(join_kernel, out, *arrays, name=f"join_{batch}")


def finish_kernel(squares, arrived, upper, lower, late, late_upper, late_lower, out):
    norm = jnp.sqrt(jnp.sum(squares[...] + arrived[2 * PART :, :], axis=0, keepdims=True))
    for first, up, low, came in ((0, upper, lower, arrived), (PART, late_upper, late_lower, late)):
        out[first : first + PART, 0, :] = (up[...] + came[:PART, :]) / norm
        out[first : first + PART, 1, :] = (low[...] + came[PART : 2 * PART, :]) / norm


def local(upper_vectors, lower_vectors, secular_roots, pole_values, pole_weights, undeflated):
    vectors = [pltpu.with_memory_space_constraint(v, pltpu.HBM) for v in (upper_vectors, lower_vectors)]
    roots = secular_roots.reshape(1, WIDE)
    sent = [pick(s, vectors[s]) for s in (0, 1)]
    raw = [exchange(sent[s], s, 0) for s in (0, 1)]
    raw[0] = pltpu.with_memory_space_constraint(raw[0], pltpu.HBM)
    packed = pack(pole_values, pole_weights, undeflated)
    poles = lax.all_to_all(packed, "row", split_axis=0, concat_axis=0, tiled=True)
    met = [exchange(poles, s, 0) for s in (0, 1)]
    *coefficients, upper_squares, lower_squares = own_loewner(roots, poles)
    own = own_products(*vectors, *coefficients)

    streams = [(s, batch) for batch in (0, 1) for s in (0, 1)]
    squares = {(s, 1): None for s in (0, 1)} | {(0, 0): upper_squares, (1, 0): lower_squares}
    send, keep, arrived, parts = {}, {}, {}, {}
    send[0, 0], parts[0], squares[0, 0], raw[0] = meet(0, raw[0], own[0], roots, met[0], squares[0, 0])
    send[1, 0], parts[1], squares[1, 0] = meet_direct(1, raw[1], own[1], roots, met[1], squares[1, 0])
    for s in (0, 1):
        send[s, 1] = add_own(768, raw[s], own[s], parts[s], name=f"meet_{s}_late")
    for s, batch in streams:
        keep[s, batch] = add_own(512 * batch, raw[s], own[s], parts[s], name=f"rest_{s}_{batch}")
    after = send[1, 1]
    for phase in (1, 2):
        for at in streams:
            arrived[at] = exchange(send[at], at[0], phase)
        for at in streams:
            half, name = PART << (3 - phase), "add_{}_{}_{}".format(phase, *at)
            send[at], keep[at], squares[at] = add(half, keep[at], arrived[at], squares[at], after, name)
            after = keep[at]
    for at in streams:
        arrived[at] = exchange(send[at], at[0], 3)
    ready = lax.ppermute(after, ("row", "col"), CORES)
    early = join(0, *(group[s, 0] for group in (keep, arrived, squares) for s in (0, 1)), ready)
    late = join(1, *(group[s, 1] for group in (keep, arrived) for s in (0, 1)), early[1])
    return call(
        finish_kernel,
        jax.ShapeDtypeStruct((ROWS, 2, WIDE), F32),
        early[3],
        exchange(early[0], 0, 4),
        *early[1:3],
        exchange(late[0], 0, 4),
        *late[1:3],
        name="finish",
    )


def solution(mesh):
    return jax.shard_map(
        local,
        mesh=mesh,
        in_specs=(
            P("row", "col"),
            P("row", "col"),
            P(),
            P(None, ("col", "row")),
            P(None, ("col", "row")),
            P(None, ("col", "row")),
        ),
        out_specs=P(("row", "col"), None, None),
        check_vma=False,
    )
```

```python
import functools

import jax
import jax.numpy as jnp
from jax import lax
from jax.experimental import pallas as pl
from jax.experimental.pallas import tpu as pltpu
from jax.sharding import PartitionSpec as P

F32 = jnp.float32
BF16 = jnp.bfloat16
ROWS = 64
PART = 32
WIDE = 512
HBM = pl.BlockSpec(memory_space=pltpu.HBM)
VMEM = pl.BlockSpec(memory_space=pltpu.VMEM)
KERNEL = pltpu.CompilerParams(vmem_limit_bytes=16 << 20)


def pair_e(x):
    return x ^ 1


def pair_f(x):
    return (((x + 1) ^ 1) + 3) & 3


def pair_a(z):
    return z ^ 1


def pair_b(z):
    return (((z + 1) ^ 1) + 7) & 7


def pair_c(z):
    return (11 + 4 * (((z + 1) >> 1) & 1) - z) & 7


def pair_d(z):
    return (13 - 4 * ((z >> 1) & 1) - z) & 7


STEPS = (
    (
        (("z", pair_a), ("z", pair_b), ("x", pair_f), ("x", pair_e), ("z", pair_c)),
        (("z", pair_b), ("z", pair_a), ("x", pair_e), ("x", pair_f), ("z", pair_d)),
    ),
    (
        (("x", pair_e), ("x", pair_f), ("z", pair_a), ("z", pair_b), ("z", pair_c)),
        (("x", pair_f), ("x", pair_e), ("z", pair_b), ("z", pair_a), ("z", pair_d)),
    ),
)


def partners(stream, phase):
    pairs = []
    for row in range(8):
        for col in range(32):
            axis, pair = STEPS[stream][row % 2][phase]
            z, x = divmod(col, 4)
            to = z * 4 + pair(x) if axis == "x" else pair(z) * 4 + x
            pairs.append((row * 32 + col, row * 32 + to))
    return pairs


CORES = [(device, device ^ 32) for device in range(256)]
PARTNERS = tuple(tuple(partners(stream, phase) for phase in range(5)) for stream in range(2))


def exchange(block, stream, phase):
    return lax.ppermute(block, ("row", "col"), PARTNERS[stream][phase])


def chunk_order(stream, count, first):
    core = lax.axis_index("row") & 1
    col = lax.axis_index("col")
    known = {}

    def place(side, axis, bits):
        key = (side, axis, bits)
        if key not in known:
            if not bits:
                known[key] = (col >> 2) if axis == "z" else (col & 3)
            else:
                pairs = [pair for on, pair in STEPS[stream][side] if on == axis]
                before = place(side, axis, bits[:-1])
                known[key] = pairs[len(bits) - 1](before) if bits[-1] else before
        return known[key]

    order = []
    for k in range(first, first + count):
        taken = [(k >> shift) & 1 for shift in (4, 3, 2, 1, 0)]
        on = []
        for side in (0, 1):
            bits = {
                axis: tuple(bit for bit, (at, _) in zip(taken, STEPS[stream][side]) if at == axis)
                for axis in ("x", "z")
            }
            on.append(place(side, "z", bits["z"]) * 4 + place(side, "x", bits["x"]))
        order.append(jnp.where(core == 0, on[0], on[1]))
    return order


def copy_rows(stream, first, vectors, out, sems):
    order = chunk_order(stream, 16, first)
    copies = []
    for n in range(32):
        batch, k = divmod(n, 16)
        at = pl.multiple_of(order[k] * ROWS + batch * PART, PART)
        copies.append(
            pltpu.make_async_copy(
                vectors.at[pl.ds(at, PART), :], out.at[pl.ds(n * PART, PART), :], sems.at[n]
            )
        )
    return copies


def pick_kernel(stream, vectors, out, rows, sems):
    arriving = copy_rows(stream, 16, vectors, rows, sems.at[0])
    for copy in arriving:
        copy.start()
    leaving = []
    for k, copy in enumerate(arriving):
        copy.wait()
        at = pl.ds(k * PART, PART)
        leaving.append(pltpu.make_async_copy(rows.at[at, :], out.at[at, :], sems.at[1, k]))
        leaving[k].start()
    for copy in leaving:
        copy.wait()


def pick(stream, vectors):
    return pl.pallas_call(
        functools.partial(pick_kernel, stream),
        out_shape=jax.ShapeDtypeStruct((16 * ROWS, WIDE), F32),
        in_specs=[HBM],
        out_specs=HBM,
        scratch_shapes=[pltpu.VMEM((16 * ROWS, WIDE), F32), pltpu.SemaphoreType.DMA((2, 32))],
        compiler_params=pltpu.CompilerParams(vmem_limit_bytes=4 << 20),
        cost_estimate=pl.CostEstimate(flops=0, bytes_accessed=4 << 20, transcendentals=0),
        name=f"pick_{stream}",
    )(vectors)


def pack_kernel(poles, weights, undeflated, out):
    out[...] = jnp.zeros_like(out)
    scaled = weights[...] * undeflated[...].astype(F32)
    for r in range(8):
        out[8 * r : 8 * r + 2, 0:64] = poles[...]
        out[8 * r + 2 : 8 * r + 4, 0:64] = scaled


def pack(*arrays):
    return pl.pallas_call(
        pack_kernel,
        out_shape=jax.ShapeDtypeStruct((64, 128), F32),
        in_specs=[VMEM] * 3,
        out_specs=VMEM,
        name="pack",
    )(*arrays)


def loewner(half, root, poles, out):
    columns = poles.T
    total = jnp.zeros((8, WIDE), F32)
    for r in range(8):
        at = 8 * r + half
        value = columns[0:64, at + 2 : at + 3] / (columns[0:64, at : at + 1] - root)
        high = value.astype(BF16)
        rows = slice(r * 64, r * 64 + 64)
        out[0, rows, :] = high
        out[1, rows, :] = (value - high.astype(F32)).astype(BF16)
        total = total + jnp.sum((value * value).reshape(8, 8, WIDE), axis=0)
    return total


COEFFICIENT = jax.ShapeDtypeStruct((2, WIDE, WIDE), BF16)
SQUARES = jax.ShapeDtypeStruct((8, WIDE), F32)


def own_loewner_kernel(roots, poles, upper, lower, upper_squares, lower_squares):
    upper_squares[...] = loewner(0, roots[...], poles[...], upper)
    lower_squares[...] = loewner(1, roots[...], poles[...], lower)


def own_loewner(roots, poles):
    return pl.pallas_call(
        own_loewner_kernel,
        out_shape=[COEFFICIENT, COEFFICIENT, SQUARES, SQUARES],
        in_specs=[VMEM] * 2,
        out_specs=[VMEM] * 4,
        compiler_params=KERNEL,
        cost_estimate=pl.CostEstimate(flops=1 << 23, bytes_accessed=2 << 20, transcendentals=1 << 19),
        name="loewner",
    )(roots, poles)


def product(vectors, high, low):
    a = vectors.astype(BF16)
    rest = (vectors - a.astype(F32)).astype(BF16)
    dot = functools.partial(jnp.dot, preferred_element_type=F32)
    return dot(a, high) + (dot(a, low) + dot(rest, high))


def own_kernel(upper, lower, upper_part, lower_part, upper_out, lower_out, rows, sems):
    streams = ((upper, upper_part, upper_out), (lower, lower_part, lower_out))
    copies = [copy_rows(s, 0, streams[s][0], rows.at[s], sems.at[s]) for s in (0, 1)]
    for copy in copies[0] + copies[1]:
        copy.start()
    for s, (_, part, out) in enumerate(streams):
        for k in range(0, 32, 8):
            for copy in copies[s][k : k + 8]:
                copy.wait()
            at = slice(k * PART, k * PART + 256)
            out[at, :] = product(rows[s, at, :], part[0], part[1])


def own_products(upper, lower, upper_part, lower_part):
    out = jax.ShapeDtypeStruct((16 * ROWS, WIDE), F32)
    return pl.pallas_call(
        own_kernel,
        out_shape=[out, out],
        in_specs=[HBM] * 2 + [VMEM] * 2,
        out_specs=[VMEM] * 2,
        scratch_shapes=[pltpu.VMEM((2, 16 * ROWS, WIDE), F32), pltpu.SemaphoreType.DMA((2, 32))],
        compiler_params=KERNEL,
        cost_estimate=pl.CostEstimate(flops=6 << 30, bytes_accessed=8 << 20, transcendentals=0),
        name="own",
    )(upper, lower, upper_part, lower_part)


def shape(rows, squares=False):
    return jax.ShapeDtypeStruct((rows + 8 if squares else rows, WIDE), F32)


def call(kernel, out_shape, *arrays, name, flops=0, from_hbm=None, scratch=()):
    return pl.pallas_call(
        kernel,
        out_shape=out_shape,
        in_specs=[HBM if n == from_hbm else VMEM for n in range(len(arrays))],
        out_specs=jax.tree.map(lambda _: VMEM, out_shape),
        scratch_shapes=scratch,
        compiler_params=KERNEL,
        cost_estimate=pl.CostEstimate(flops=flops, bytes_accessed=1 << 20, transcendentals=0),
        name=name,
    )(*arrays)


def meet_kernel(stream, vectors, own, roots, poles, squares, send, coefficient, sums, rows, sems):
    copies = []
    for n, first in enumerate((256, 768, 0, 512)):
        at = pl.ds(first, 256)
        copies.append(pltpu.make_async_copy(vectors.at[at, :], rows.at[at, :], sems.at[n]))
        copies[n].start()
    total = squares[...] + loewner(stream, roots[...], poles[...], coefficient)
    send[256:, :] = total
    sums[...] = total
    copies[0].wait()
    send[:256, :] = own[256:512, :] + product(rows[256:512, :], coefficient[0], coefficient[1])
    for copy in copies[1:]:
        copy.wait()


def meet_direct(stream, *arrays):
    return call(
        functools.partial(meet_direct_kernel, stream),
        [shape(256, True), COEFFICIENT, SQUARES],
        *arrays,
        name=f"meet_{stream}",
        flops=1 << 30,
    )


def meet(stream, *arrays):
    return call(
        functools.partial(meet_kernel, stream),
        [shape(256, True), COEFFICIENT, SQUARES, shape(16 * ROWS)],
        *arrays,
        name=f"meet_{stream}",
        flops=1 << 30,
        from_hbm=0,
        scratch=[pltpu.SemaphoreType.DMA((4,))],
    )


def meet_direct_kernel(stream, vectors, own, roots, poles, squares, send, coefficient, sums):
    total = squares[...] + loewner(stream, roots[...], poles[...], coefficient)
    send[256:, :] = total
    sums[...] = total
    send[:256, :] = own[256:512, :] + product(vectors[256:512, :], coefficient[0], coefficient[1])


def add_own_kernel(first, vectors, own, coefficient, out):
    at = slice(first, first + 256)
    out[...] = own[at, :] + product(vectors[at, :], coefficient[0], coefficient[1])


def add_own(first, *arrays, name):
    return call(functools.partial(add_own_kernel, first), shape(256), *arrays, name=name, flops=1 << 30)


def add_kernel(half, kept, arrived, *refs):
    if len(refs) > 3:
        squares, _, send, keep, sums = refs
        total = squares[...] + arrived[2 * half :, :]
        send[half:, :] = total
        sums[...] = total
    else:
        _, send, keep = refs
    send[:half, :] = kept[half:, :] + arrived[half : 2 * half, :]
    keep[...] = kept[:half, :] + arrived[:half, :]


def add(half, kept, arrived, squares, after, name):
    kernel = functools.partial(add_kernel, half)
    if squares is None:
        return *call(kernel, [shape(half), shape(half)], kept, arrived, after, name=name), None
    return call(kernel, [shape(half, True), shape(half), SQUARES], kept, arrived, squares, after, name=name)


def join_kernel(upper, lower, upper_in, lower_in, *refs):
    if len(refs) > 4:
        upper_squares, lower_squares, _, send, up, low, sums = refs
        total = upper_squares[...] + lower_squares[...]
        total = total + (upper_in[2 * PART :, :] + lower_in[2 * PART :, :])
        send[2 * PART :, :] = total
        sums[...] = total
    else:
        _, send, up, low = refs
    send[:PART, :] = upper[PART:, :] + upper_in[PART : 2 * PART, :]
    send[PART : 2 * PART, :] = lower[PART:, :] + lower_in[PART : 2 * PART, :]
    up[...] = upper[:PART, :] + upper_in[:PART, :]
    low[...] = lower[:PART, :] + lower_in[:PART, :]


def join(batch, *arrays):
    out = [shape(2 * PART, batch == 0), shape(PART), shape(PART)] + [SQUARES] * (batch == 0)
    return call(join_kernel, out, *arrays, name=f"join_{batch}")


def finish_kernel(squares, arrived, upper, lower, late, late_upper, late_lower, out):
    norm = jnp.sqrt(jnp.sum(squares[...] + arrived[2 * PART :, :], axis=0, keepdims=True))
    for first, up, low, came in ((0, upper, lower, arrived), (PART, late_upper, late_lower, late)):
        out[first : first + PART, 0, :] = (up[...] + came[:PART, :]) / norm
        out[first : first + PART, 1, :] = (low[...] + came[PART : 2 * PART, :]) / norm


def local(upper_vectors, lower_vectors, secular_roots, pole_values, pole_weights, undeflated):
    vectors = [pltpu.with_memory_space_constraint(v, pltpu.HBM) for v in (upper_vectors, lower_vectors)]
    roots = secular_roots.reshape(1, WIDE)
    sent = [pick(s, vectors[s]) for s in (0, 1)]
    raw = [exchange(sent[s], s, 0) for s in (0, 1)]
    raw[0] = pltpu.with_memory_space_constraint(raw[0], pltpu.HBM)
    packed = pack(pole_values, pole_weights, undeflated)
    poles = lax.all_to_all(packed, "row", split_axis=0, concat_axis=0, tiled=True)
    met = [exchange(poles, s, 0) for s in (0, 1)]
    *coefficients, upper_squares, lower_squares = own_loewner(roots, poles)
    own = own_products(*vectors, *coefficients)

    streams = [(s, batch) for batch in (0, 1) for s in (0, 1)]
    squares = {(s, 1): None for s in (0, 1)} | {(0, 0): upper_squares, (1, 0): lower_squares}
    send, keep, arrived, parts = {}, {}, {}, {}
    send[0, 0], parts[0], squares[0, 0], raw[0] = meet(0, raw[0], own[0], roots, met[0], squares[0, 0])
    send[1, 0], parts[1], squares[1, 0] = meet_direct(1, raw[1], own[1], roots, met[1], squares[1, 0])
    for s in (0, 1):
        send[s, 1] = add_own(768, raw[s], own[s], parts[s], name=f"meet_{s}_late")
    for s, batch in streams:
        keep[s, batch] = add_own(512 * batch, raw[s], own[s], parts[s], name=f"rest_{s}_{batch}")
    after = send[1, 1]
    for phase in (1, 2):
        for at in streams:
            arrived[at] = exchange(send[at], at[0], phase)
        for at in sorted(streams) if phase == 1 else streams:
            half, name = PART << (3 - phase), "add_{}_{}_{}".format(phase, *at)
            send[at], keep[at], squares[at] = add(half, keep[at], arrived[at], squares[at], after, name)
            after = keep[at]
    for at in streams:
        arrived[at] = exchange(send[at], at[0], 3)
    ready = lax.ppermute(after, ("row", "col"), CORES)
    early = join(0, *(group[s, 0] for group in (keep, arrived, squares) for s in (0, 1)), ready)
    late = join(1, *(group[s, 1] for group in (keep, arrived) for s in (0, 1)), early[1])
    return call(
        finish_kernel,
        jax.ShapeDtypeStruct((ROWS, 2, WIDE), F32),
        early[3],
        exchange(early[0], 0, 4),
        *early[1:3],
        exchange(late[0], 0, 4),
        *late[1:3],
        name="finish",
    )


def solution(mesh):
    return jax.shard_map(
        local,
        mesh=mesh,
        in_specs=(
            P("row", "col"),
            P("row", "col"),
            P(),
            P(None, ("col", "row")),
            P(None, ("col", "row")),
            P(None, ("col", "row")),
        ),
        out_specs=P(("row", "col"), None, None),
        check_vma=False,
    )
```

```python
import functools

import jax
import jax.numpy as jnp
from jax import lax
from jax.experimental import pallas as pl
from jax.experimental.pallas import tpu as pltpu
from jax.sharding import PartitionSpec as P

F32 = jnp.float32
BF16 = jnp.bfloat16
ROWS = 64
PART = 32
WIDE = 512
HBM = pl.BlockSpec(memory_space=pltpu.HBM)
VMEM = pl.BlockSpec(memory_space=pltpu.VMEM)
KERNEL = pltpu.CompilerParams(vmem_limit_bytes=16 << 20)


def pair_e(x):
    return x ^ 1


def pair_f(x):
    return (((x + 1) ^ 1) + 3) & 3


def pair_a(z):
    return z ^ 1


def pair_b(z):
    return (((z + 1) ^ 1) + 7) & 7


def pair_c(z):
    return (11 + 4 * (((z + 1) >> 1) & 1) - z) & 7


def pair_d(z):
    return (13 - 4 * ((z >> 1) & 1) - z) & 7


STEPS = (
    (
        (("z", pair_a), ("z", pair_b), ("x", pair_f), ("x", pair_e), ("z", pair_c)),
        (("z", pair_b), ("z", pair_a), ("x", pair_e), ("x", pair_f), ("z", pair_d)),
    ),
    (
        (("x", pair_e), ("x", pair_f), ("z", pair_a), ("z", pair_b), ("z", pair_c)),
        (("x", pair_f), ("x", pair_e), ("z", pair_b), ("z", pair_a), ("z", pair_d)),
    ),
)


def partners(stream, phase):
    pairs = []
    for row in range(8):
        for col in range(32):
            axis, pair = STEPS[stream][row % 2][phase]
            z, x = divmod(col, 4)
            to = z * 4 + pair(x) if axis == "x" else pair(z) * 4 + x
            pairs.append((row * 32 + col, row * 32 + to))
    return pairs


CORES = [(device, device ^ 32) for device in range(256)]
PARTNERS = tuple(tuple(partners(stream, phase) for phase in range(5)) for stream in range(2))


POLES = tuple([(source ^ 32, to) for source, to in PARTNERS[stream][0]] for stream in range(2))


def exchange(block, stream, phase):
    return lax.ppermute(block, ("row", "col"), PARTNERS[stream][phase])


def chunk_order(stream, count, first):
    core = lax.axis_index("row") & 1
    col = lax.axis_index("col")
    known = {}

    def place(side, axis, bits):
        key = (side, axis, bits)
        if key not in known:
            if not bits:
                known[key] = (col >> 2) if axis == "z" else (col & 3)
            else:
                pairs = [pair for on, pair in STEPS[stream][side] if on == axis]
                before = place(side, axis, bits[:-1])
                known[key] = pairs[len(bits) - 1](before) if bits[-1] else before
        return known[key]

    order = []
    for k in range(first, first + count):
        taken = [(k >> shift) & 1 for shift in (4, 3, 2, 1, 0)]
        on = []
        for side in (0, 1):
            bits = {
                axis: tuple(bit for bit, (at, _) in zip(taken, STEPS[stream][side]) if at == axis)
                for axis in ("x", "z")
            }
            on.append(place(side, "z", bits["z"]) * 4 + place(side, "x", bits["x"]))
        order.append(jnp.where(core == 0, on[0], on[1]))
    return order


def copy_rows(stream, first, vectors, out, sems):
    order = chunk_order(stream, 16, first)
    copies = []
    for n in range(32):
        batch, k = divmod(n, 16)
        at = pl.multiple_of(order[k] * ROWS + batch * PART, PART)
        copies.append(
            pltpu.make_async_copy(
                vectors.at[pl.ds(at, PART), :], out.at[pl.ds(n * PART, PART), :], sems.at[n]
            )
        )
    return copies


def pick_kernel(stream, vectors, out, rows, sems):
    arriving = copy_rows(stream, 16, vectors, rows, sems.at[0])
    for copy in arriving:
        copy.start()
    leaving = []
    for k, copy in enumerate(arriving):
        copy.wait()
        at = pl.ds(k * PART, PART)
        leaving.append(pltpu.make_async_copy(rows.at[at, :], out.at[at, :], sems.at[1, k]))
        leaving[k].start()
    for copy in leaving:
        copy.wait()


def pick(stream, vectors):
    return pl.pallas_call(
        functools.partial(pick_kernel, stream),
        out_shape=jax.ShapeDtypeStruct((16 * ROWS, WIDE), F32),
        in_specs=[HBM],
        out_specs=HBM,
        scratch_shapes=[pltpu.VMEM((16 * ROWS, WIDE), F32), pltpu.SemaphoreType.DMA((2, 32))],
        compiler_params=pltpu.CompilerParams(vmem_limit_bytes=4 << 20),
        cost_estimate=pl.CostEstimate(flops=0, bytes_accessed=4 << 20, transcendentals=0),
        name=f"pick_{stream}",
    )(vectors)


def pack_kernel(poles, weights, undeflated, out):
    out[...] = jnp.zeros_like(out)
    scaled = weights[...] * undeflated[...].astype(F32)
    for r in range(8):
        out[8 * r : 8 * r + 2, 0:64] = poles[...]
        out[8 * r + 2 : 8 * r + 4, 0:64] = scaled


def pack(*arrays):
    return pl.pallas_call(
        pack_kernel,
        out_shape=jax.ShapeDtypeStruct((64, 128), F32),
        in_specs=[VMEM] * 3,
        out_specs=VMEM,
        name="pack",
    )(*arrays)


def loewner(half, root, poles, out):
    columns = poles.T
    total = jnp.zeros((8, WIDE), F32)
    for r in range(8):
        at = 8 * r + half
        value = columns[0:64, at + 2 : at + 3] / (columns[0:64, at : at + 1] - root)
        high = value.astype(BF16)
        rows = slice(r * 64, r * 64 + 64)
        out[0, rows, :] = high
        out[1, rows, :] = (value - high.astype(F32)).astype(BF16)
        total = total + jnp.sum((value * value).reshape(8, 8, WIDE), axis=0)
    return total


COEFFICIENT = jax.ShapeDtypeStruct((2, WIDE, WIDE), BF16)
SQUARES = jax.ShapeDtypeStruct((8, WIDE), F32)


def own_loewner_kernel(roots, poles, upper, lower, upper_squares, lower_squares):
    upper_squares[...] = loewner(0, roots[...], poles[...], upper)
    lower_squares[...] = loewner(1, roots[...], poles[...], lower)


def own_loewner(roots, poles):
    return pl.pallas_call(
        own_loewner_kernel,
        out_shape=[COEFFICIENT, COEFFICIENT, SQUARES, SQUARES],
        in_specs=[VMEM] * 2,
        out_specs=[VMEM] * 4,
        compiler_params=KERNEL,
        cost_estimate=pl.CostEstimate(flops=1 << 23, bytes_accessed=2 << 20, transcendentals=1 << 19),
        name="loewner",
    )(roots, poles)


def partner_loewner_kernel(
    roots, to_upper, to_lower, upper_own, lower_own, _, upper, lower, upper_squares, lower_squares
):
    upper_squares[...] = upper_own[...] + loewner(0, roots[...], to_upper[...], upper)
    lower_squares[...] = lower_own[...] + loewner(1, roots[...], to_lower[...], lower)


def partner_loewner(*arrays):
    return pl.pallas_call(
        partner_loewner_kernel,
        out_shape=[COEFFICIENT, COEFFICIENT, SQUARES, SQUARES],
        in_specs=[VMEM] * 6,
        out_specs=[VMEM] * 4,
        compiler_params=KERNEL,
        cost_estimate=pl.CostEstimate(flops=1 << 23, bytes_accessed=2 << 20, transcendentals=1 << 19),
        name="partner",
    )(*arrays)


def product(vectors, high, low):
    a = vectors.astype(BF16)
    rest = (vectors - a.astype(F32)).astype(BF16)
    dot = functools.partial(jnp.dot, preferred_element_type=F32)
    return dot(a, high) + (dot(a, low) + dot(rest, high))


def own_kernel(upper, lower, upper_part, lower_part, upper_out, lower_out, rows, sems):
    streams = ((upper, upper_part, upper_out), (lower, lower_part, lower_out))
    copies = [copy_rows(s, 0, streams[s][0], rows.at[s], sems.at[s]) for s in (0, 1)]
    for copy in copies[0] + copies[1]:
        copy.start()
    for s, (_, part, out) in enumerate(streams):
        for k in range(0, 32, 8):
            for copy in copies[s][k : k + 8]:
                copy.wait()
            at = slice(k * PART, k * PART + 256)
            out[at, :] = product(rows[s, at, :], part[0], part[1])


def own_products(upper, lower, upper_part, lower_part):
    out = jax.ShapeDtypeStruct((16 * ROWS, WIDE), F32)
    return pl.pallas_call(
        own_kernel,
        out_shape=[out, out],
        in_specs=[HBM] * 2 + [VMEM] * 2,
        out_specs=[VMEM] * 2,
        scratch_shapes=[pltpu.VMEM((2, 16 * ROWS, WIDE), F32), pltpu.SemaphoreType.DMA((2, 32))],
        compiler_params=KERNEL,
        cost_estimate=pl.CostEstimate(flops=6 << 30, bytes_accessed=8 << 20, transcendentals=0),
        name="own",
    )(upper, lower, upper_part, lower_part)


def shape(rows, squares=False):
    return jax.ShapeDtypeStruct((rows + 8 if squares else rows, WIDE), F32)


def call(kernel, out_shape, *arrays, name, flops=0, from_hbm=None, scratch=()):
    return pl.pallas_call(
        kernel,
        out_shape=out_shape,
        in_specs=[HBM if n == from_hbm else VMEM for n in range(len(arrays))],
        out_specs=jax.tree.map(lambda _: VMEM, out_shape),
        scratch_shapes=scratch,
        compiler_params=KERNEL,
        cost_estimate=pl.CostEstimate(flops=flops, bytes_accessed=1 << 20, transcendentals=0),
        name=name,
    )(*arrays)


def meet_kernel(vectors, own, coefficient, squares, send, rows, sems):
    copies = []
    for n, first in enumerate((256, 768, 0, 512)):
        at = pl.ds(first, 256)
        copies.append(pltpu.make_async_copy(vectors.at[at, :], rows.at[at, :], sems.at[n]))
        copies[n].start()
    send[256:, :] = squares[...]
    copies[0].wait()
    send[:256, :] = own[256:512, :] + product(rows[256:512, :], coefficient[0], coefficient[1])
    for copy in copies[1:]:
        copy.wait()


def meet_direct_kernel(vectors, own, coefficient, squares, send):
    send[256:, :] = squares[...]
    send[:256, :] = own[256:512, :] + product(vectors[256:512, :], coefficient[0], coefficient[1])


def meet(*arrays):
    return call(
        meet_kernel,
        [shape(256, True), shape(16 * ROWS)],
        *arrays,
        name="meet_0",
        flops=1 << 30,
        from_hbm=0,
        scratch=[pltpu.SemaphoreType.DMA((4,))],
    )


def meet_direct(*arrays):
    return call(meet_direct_kernel, shape(256, True), *arrays, name="meet_1", flops=1 << 30)


def add_own_kernel(first, vectors, own, coefficient, out):
    at = slice(first, first + 256)
    out[...] = own[at, :] + product(vectors[at, :], coefficient[0], coefficient[1])


def add_own(first, *arrays, name):
    return call(functools.partial(add_own_kernel, first), shape(256), *arrays, name=name, flops=1 << 30)


def add_kernel(half, kept, arrived, *refs):
    if len(refs) > 3:
        squares, _, send, keep, sums = refs
        total = squares[...] + arrived[2 * half :, :]
        send[half:, :] = total
        sums[...] = total
    else:
        _, send, keep = refs
    send[:half, :] = kept[half:, :] + arrived[half : 2 * half, :]
    keep[...] = kept[:half, :] + arrived[:half, :]


def add(half, kept, arrived, squares, after, name):
    kernel = functools.partial(add_kernel, half)
    if squares is None:
        return *call(kernel, [shape(half), shape(half)], kept, arrived, after, name=name), None
    return call(kernel, [shape(half, True), shape(half), SQUARES], kept, arrived, squares, after, name=name)


def join_kernel(upper, lower, upper_in, lower_in, *refs):
    if len(refs) > 4:
        upper_squares, lower_squares, _, send, up, low, sums = refs
        total = upper_squares[...] + lower_squares[...]
        total = total + (upper_in[2 * PART :, :] + lower_in[2 * PART :, :])
        send[2 * PART :, :] = total
        sums[...] = total
    else:
        _, send, up, low = refs
    send[:PART, :] = upper[PART:, :] + upper_in[PART : 2 * PART, :]
    send[PART : 2 * PART, :] = lower[PART:, :] + lower_in[PART : 2 * PART, :]
    up[...] = upper[:PART, :] + upper_in[:PART, :]
    low[...] = lower[:PART, :] + lower_in[:PART, :]


def join(batch, *arrays):
    out = [shape(2 * PART, batch == 0), shape(PART), shape(PART)] + [SQUARES] * (batch == 0)
    return call(join_kernel, out, *arrays, name=f"join_{batch}")


def finish_kernel(squares, arrived, upper, lower, late, late_upper, late_lower, out):
    norm = jnp.sqrt(jnp.sum(squares[...] + arrived[2 * PART :, :], axis=0, keepdims=True))
    for first, up, low, came in ((0, upper, lower, arrived), (PART, late_upper, late_lower, late)):
        out[first : first + PART, 0, :] = (up[...] + came[:PART, :]) / norm
        out[first : first + PART, 1, :] = (low[...] + came[PART : 2 * PART, :]) / norm


def local(upper_vectors, lower_vectors, secular_roots, pole_values, pole_weights, undeflated):
    vectors = [pltpu.with_memory_space_constraint(v, pltpu.HBM) for v in (upper_vectors, lower_vectors)]
    roots = secular_roots.reshape(1, WIDE)
    sent = [pick(s, vectors[s]) for s in (0, 1)]
    raw = [exchange(sent[s], s, 0) for s in (0, 1)]
    raw[0] = pltpu.with_memory_space_constraint(raw[0], pltpu.HBM)
    packed = pack(pole_values, pole_weights, undeflated)
    poles = lax.all_to_all(packed, "row", split_axis=0, concat_axis=0, tiled=True)
    met = [lax.ppermute(poles, ("row", "col"), POLES[s]) for s in (0, 1)]
    *coefficients, upper_squares, lower_squares = own_loewner(roots, poles)
    own = own_products(*vectors, *coefficients)

    streams = [(s, batch) for batch in (0, 1) for s in (0, 1)]
    squares = {(s, 1): None for s in (0, 1)} | {(0, 0): upper_squares, (1, 0): lower_squares}
    send, keep, arrived = {}, {}, {}
    *parts, squares[0, 0], squares[1, 0] = partner_loewner(roots, *met, squares[0, 0], squares[1, 0], own[1])
    send[0, 0], raw[0] = meet(raw[0], own[0], parts[0], squares[0, 0])
    send[1, 0] = meet_direct(raw[1], own[1], parts[1], squares[1, 0])
    for s in (0, 1):
        send[s, 1] = add_own(768, raw[s], own[s], parts[s], name=f"meet_{s}_late")
    for s, batch in streams:
        keep[s, batch] = add_own(512 * batch, raw[s], own[s], parts[s], name=f"rest_{s}_{batch}")
    after = send[1, 1]
    for phase in (1, 2):
        for at in streams:
            arrived[at] = exchange(send[at], at[0], phase)
        for at in sorted(streams) if phase == 1 else streams:
            half, name = PART << (3 - phase), "add_{}_{}_{}".format(phase, *at)
            send[at], keep[at], squares[at] = add(half, keep[at], arrived[at], squares[at], after, name)
            after = keep[at]
    for at in streams:
        arrived[at] = exchange(send[at], at[0], 3)
    ready = lax.ppermute(after, ("row", "col"), CORES)
    early = join(0, *(group[s, 0] for group in (keep, arrived, squares) for s in (0, 1)), ready)
    late = join(1, *(group[s, 1] for group in (keep, arrived) for s in (0, 1)), early[1])
    return call(
        finish_kernel,
        jax.ShapeDtypeStruct((ROWS, 2, WIDE), F32),
        early[3],
        exchange(early[0], 0, 4),
        *early[1:3],
        exchange(late[0], 0, 4),
        *late[1:3],
        name="finish",
    )


def solution(mesh):
    return jax.shard_map(
        local,
        mesh=mesh,
        in_specs=(
            P("row", "col"),
            P("row", "col"),
            P(),
            P(None, ("col", "row")),
            P(None, ("col", "row")),
            P(None, ("col", "row")),
        ),
        out_specs=P(("row", "col"), None, None),
        check_vma=False,
    )
```

```python
import functools

import jax
import jax.numpy as jnp
from jax import lax
from jax.experimental import pallas as pl
from jax.experimental.pallas import tpu as pltpu
from jax.sharding import PartitionSpec as P

F32 = jnp.float32
BF16 = jnp.bfloat16
ROWS = 64
PART = 32
WIDE = 512
HBM = pl.BlockSpec(memory_space=pltpu.HBM)
VMEM = pl.BlockSpec(memory_space=pltpu.VMEM)
KERNEL = pltpu.CompilerParams(vmem_limit_bytes=16 << 20)


def pair_e(x):
    return x ^ 1


def pair_f(x):
    return (((x + 1) ^ 1) + 3) & 3


def pair_a(z):
    return z ^ 1


def pair_b(z):
    return (((z + 1) ^ 1) + 7) & 7


def pair_c(z):
    return (11 + 4 * (((z + 1) >> 1) & 1) - z) & 7


def pair_d(z):
    return (13 - 4 * ((z >> 1) & 1) - z) & 7


STEPS = (
    (
        (("z", pair_a), ("z", pair_b), ("x", pair_f), ("x", pair_e), ("z", pair_c)),
        (("z", pair_b), ("z", pair_a), ("x", pair_e), ("x", pair_f), ("z", pair_d)),
    ),
    (
        (("x", pair_e), ("x", pair_f), ("z", pair_a), ("z", pair_b), ("z", pair_c)),
        (("x", pair_f), ("x", pair_e), ("z", pair_b), ("z", pair_a), ("z", pair_d)),
    ),
)


def partners(stream, phase):
    pairs = []
    for row in range(8):
        for col in range(32):
            axis, pair = STEPS[stream][row % 2][phase]
            z, x = divmod(col, 4)
            to = z * 4 + pair(x) if axis == "x" else pair(z) * 4 + x
            pairs.append((row * 32 + col, row * 32 + to))
    return pairs


CORES = [(device, device ^ 32) for device in range(256)]
PARTNERS = tuple(tuple(partners(stream, phase) for phase in range(5)) for stream in range(2))


POLES = tuple([(source ^ 32, to) for source, to in PARTNERS[stream][0]] for stream in range(2))


def exchange(block, stream, phase):
    return lax.ppermute(block, ("row", "col"), PARTNERS[stream][phase])


def chunk_order(stream, count, first):
    core = lax.axis_index("row") & 1
    col = lax.axis_index("col")
    known = {}

    def place(side, axis, bits):
        key = (side, axis, bits)
        if key not in known:
            if not bits:
                known[key] = (col >> 2) if axis == "z" else (col & 3)
            else:
                pairs = [pair for on, pair in STEPS[stream][side] if on == axis]
                before = place(side, axis, bits[:-1])
                known[key] = pairs[len(bits) - 1](before) if bits[-1] else before
        return known[key]

    order = []
    for k in range(first, first + count):
        taken = [(k >> shift) & 1 for shift in (4, 3, 2, 1, 0)]
        on = []
        for side in (0, 1):
            bits = {
                axis: tuple(bit for bit, (at, _) in zip(taken, STEPS[stream][side]) if at == axis)
                for axis in ("x", "z")
            }
            on.append(place(side, "z", bits["z"]) * 4 + place(side, "x", bits["x"]))
        order.append(jnp.where(core == 0, on[0], on[1]))
    return order


def copy_rows(stream, first, vectors, out, sems):
    order = chunk_order(stream, 16, first)
    copies = []
    for n in range(32):
        batch, k = divmod(n, 16)
        at = pl.multiple_of(order[k] * ROWS + batch * PART, PART)
        copies.append(
            pltpu.make_async_copy(
                vectors.at[pl.ds(at, PART), :], out.at[pl.ds(n * PART, PART), :], sems.at[n]
            )
        )
    return copies


def pick_kernel(stream, vectors, out, rows, sems):
    arriving = copy_rows(stream, 16, vectors, rows, sems.at[0])
    for copy in arriving:
        copy.start()
    leaving = []
    for k, copy in enumerate(arriving):
        copy.wait()
        at = pl.ds(k * PART, PART)
        leaving.append(pltpu.make_async_copy(rows.at[at, :], out.at[at, :], sems.at[1, k]))
        leaving[k].start()
    for copy in leaving:
        copy.wait()


def pick(stream, vectors):
    return pl.pallas_call(
        functools.partial(pick_kernel, stream),
        out_shape=jax.ShapeDtypeStruct((16 * ROWS, WIDE), F32),
        in_specs=[HBM],
        out_specs=HBM,
        scratch_shapes=[pltpu.VMEM((16 * ROWS, WIDE), F32), pltpu.SemaphoreType.DMA((2, 32))],
        compiler_params=pltpu.CompilerParams(vmem_limit_bytes=4 << 20),
        cost_estimate=pl.CostEstimate(flops=0, bytes_accessed=4 << 20, transcendentals=0),
        name=f"pick_{stream}",
    )(vectors)


def pack_kernel(poles, weights, undeflated, out):
    out[...] = jnp.zeros_like(out)
    scaled = weights[...] * undeflated[...].astype(F32)
    for r in range(8):
        out[8 * r : 8 * r + 2, 0:64] = poles[...]
        out[8 * r + 2 : 8 * r + 4, 0:64] = scaled


def pack(*arrays):
    return pl.pallas_call(
        pack_kernel,
        out_shape=jax.ShapeDtypeStruct((64, 128), F32),
        in_specs=[VMEM] * 3,
        out_specs=VMEM,
        name="pack",
    )(*arrays)


def loewner(half, root, poles, out):
    columns = poles.T
    total = jnp.zeros((8, WIDE), F32)
    for r in range(8):
        at = 8 * r + half
        value = columns[0:64, at + 2 : at + 3] / (columns[0:64, at : at + 1] - root)
        high = value.astype(BF16)
        rows = slice(r * 64, r * 64 + 64)
        out[0, rows, :] = high
        out[1, rows, :] = (value - high.astype(F32)).astype(BF16)
        total = total + jnp.sum((value * value).reshape(8, 8, WIDE), axis=0)
    return total


COEFFICIENT = jax.ShapeDtypeStruct((2, WIDE, WIDE), BF16)
SQUARES = jax.ShapeDtypeStruct((8, WIDE), F32)


def own_loewner_kernel(roots, poles, upper, lower, upper_squares, lower_squares):
    upper_squares[...] = loewner(0, roots[...], poles[...], upper)
    lower_squares[...] = loewner(1, roots[...], poles[...], lower)


def own_loewner(roots, poles):
    return pl.pallas_call(
        own_loewner_kernel,
        out_shape=[COEFFICIENT, COEFFICIENT, SQUARES, SQUARES],
        in_specs=[VMEM] * 2,
        out_specs=[VMEM] * 4,
        compiler_params=KERNEL,
        cost_estimate=pl.CostEstimate(flops=1 << 23, bytes_accessed=2 << 20, transcendentals=1 << 19),
        name="loewner",
    )(roots, poles)


def partner_loewner_kernel(
    roots, to_upper, to_lower, upper_own, lower_own, _, upper, lower, upper_squares, lower_squares
):
    upper_squares[...] = upper_own[...] + loewner(0, roots[...], to_upper[...], upper)
    lower_squares[...] = lower_own[...] + loewner(1, roots[...], to_lower[...], lower)


def partner_loewner(*arrays):
    return pl.pallas_call(
        partner_loewner_kernel,
        out_shape=[COEFFICIENT, COEFFICIENT, SQUARES, SQUARES],
        in_specs=[VMEM] * 6,
        out_specs=[VMEM] * 4,
        compiler_params=KERNEL,
        cost_estimate=pl.CostEstimate(flops=1 << 23, bytes_accessed=2 << 20, transcendentals=1 << 19),
        name="partner",
    )(*arrays)


def product(vectors, high, low):
    a = vectors.astype(BF16)
    rest = (vectors - a.astype(F32)).astype(BF16)
    dot = functools.partial(jnp.dot, preferred_element_type=F32)
    return dot(a, high) + (dot(a, low) + dot(rest, high))


def own_kernel(upper, lower, upper_part, lower_part, upper_out, lower_out, rows, sems):
    streams = ((upper, upper_part, upper_out), (lower, lower_part, lower_out))
    copies = [copy_rows(s, 0, streams[s][0], rows.at[s], sems.at[s]) for s in (0, 1)]
    for copy in copies[0] + copies[1]:
        copy.start()
    for s, (_, part, out) in enumerate(streams):
        for k in range(0, 32, 8):
            for copy in copies[s][k : k + 8]:
                copy.wait()
            at = slice(k * PART, k * PART + 256)
            out[at, :] = product(rows[s, at, :], part[0], part[1])


def own_products(upper, lower, upper_part, lower_part):
    out = jax.ShapeDtypeStruct((16 * ROWS, WIDE), F32)
    return pl.pallas_call(
        own_kernel,
        out_shape=[out, out],
        in_specs=[HBM] * 2 + [VMEM] * 2,
        out_specs=[VMEM] * 2,
        scratch_shapes=[pltpu.VMEM((2, 16 * ROWS, WIDE), F32), pltpu.SemaphoreType.DMA((2, 32))],
        compiler_params=KERNEL,
        cost_estimate=pl.CostEstimate(flops=6 << 30, bytes_accessed=8 << 20, transcendentals=0),
        name="own",
    )(upper, lower, upper_part, lower_part)


def shape(rows, squares=False):
    return jax.ShapeDtypeStruct((rows + 8 if squares else rows, WIDE), F32)


def call(kernel, out_shape, *arrays, name, flops=0, from_hbm=None, scratch=()):
    return pl.pallas_call(
        kernel,
        out_shape=out_shape,
        in_specs=[HBM if n == from_hbm else VMEM for n in range(len(arrays))],
        out_specs=jax.tree.map(lambda _: VMEM, out_shape),
        scratch_shapes=scratch,
        compiler_params=KERNEL,
        cost_estimate=pl.CostEstimate(flops=flops, bytes_accessed=1 << 20, transcendentals=0),
        name=name,
    )(*arrays)


def meet_kernel(vectors, own, coefficient, squares, send, rows, sems):
    copies = []
    for n, first in enumerate((256, 768, 0, 512)):
        at = pl.ds(first, 256)
        copies.append(pltpu.make_async_copy(vectors.at[at, :], rows.at[at, :], sems.at[n]))
        copies[n].start()
    send[256:, :] = squares[...]
    copies[0].wait()
    send[:256, :] = own[256:512, :] + product(rows[256:512, :], coefficient[0], coefficient[1])
    for copy in copies[1:]:
        copy.wait()


def meet_direct_kernel(vectors, own, coefficient, squares, send):
    send[256:, :] = squares[...]
    send[:256, :] = own[256:512, :] + product(vectors[256:512, :], coefficient[0], coefficient[1])


def meet(*arrays):
    return call(
        meet_kernel,
        [shape(256, True), shape(16 * ROWS)],
        *arrays,
        name="meet_0",
        flops=1 << 30,
        from_hbm=0,
        scratch=[pltpu.SemaphoreType.DMA((4,))],
    )


def meet_direct(*arrays):
    return call(meet_direct_kernel, shape(256, True), *arrays, name="meet_1", flops=1 << 30)


def add_own_kernel(first, vectors, own, coefficient, *refs):
    out = refs[-1]
    at = slice(first, first + 256)
    out[...] = own[at, :] + product(vectors[at, :], coefficient[0], coefficient[1])


def add_own(first, *arrays, name):
    return call(functools.partial(add_own_kernel, first), shape(256), *arrays, name=name, flops=1 << 30)


def add_kernel(half, kept, arrived, *refs):
    if len(refs) > 3:
        squares, _, send, keep, sums = refs
        total = squares[...] + arrived[2 * half :, :]
        send[half:, :] = total
        sums[...] = total
    else:
        _, send, keep = refs
    send[:half, :] = kept[half:, :] + arrived[half : 2 * half, :]
    keep[...] = kept[:half, :] + arrived[:half, :]


def add(half, kept, arrived, squares, after, name):
    kernel = functools.partial(add_kernel, half)
    if squares is None:
        return *call(kernel, [shape(half), shape(half)], kept, arrived, after, name=name), None
    return call(kernel, [shape(half, True), shape(half), SQUARES], kept, arrived, squares, after, name=name)


def join_kernel(upper, lower, upper_in, lower_in, *refs):
    if len(refs) > 4:
        upper_squares, lower_squares, _, send, up, low, sums = refs
        total = upper_squares[...] + lower_squares[...]
        total = total + (upper_in[2 * PART :, :] + lower_in[2 * PART :, :])
        send[2 * PART :, :] = total
        sums[...] = total
    else:
        _, send, up, low = refs
    send[:PART, :] = upper[PART:, :] + upper_in[PART : 2 * PART, :]
    send[PART : 2 * PART, :] = lower[PART:, :] + lower_in[PART : 2 * PART, :]
    up[...] = upper[:PART, :] + upper_in[:PART, :]
    low[...] = lower[:PART, :] + lower_in[:PART, :]


def join(batch, *arrays):
    out = [shape(2 * PART, batch == 0), shape(PART), shape(PART)] + [SQUARES] * (batch == 0)
    return call(join_kernel, out, *arrays, name=f"join_{batch}")


def finish_kernel(squares, arrived, upper, lower, late, late_upper, late_lower, out):
    norm = jnp.sqrt(jnp.sum(squares[...] + arrived[2 * PART :, :], axis=0, keepdims=True))
    for first, up, low, came in ((0, upper, lower, arrived), (PART, late_upper, late_lower, late)):
        out[first : first + PART, 0, :] = (up[...] + came[:PART, :]) / norm
        out[first : first + PART, 1, :] = (low[...] + came[PART : 2 * PART, :]) / norm


def local(upper_vectors, lower_vectors, secular_roots, pole_values, pole_weights, undeflated):
    vectors = [pltpu.with_memory_space_constraint(v, pltpu.HBM) for v in (upper_vectors, lower_vectors)]
    roots = secular_roots.reshape(1, WIDE)
    sent = [pick(s, vectors[s]) for s in (0, 1)]
    raw = [exchange(sent[s], s, 0) for s in (0, 1)]
    raw[0] = pltpu.with_memory_space_constraint(raw[0], pltpu.HBM)
    packed = pack(pole_values, pole_weights, undeflated)
    poles = lax.all_to_all(packed, "row", split_axis=0, concat_axis=0, tiled=True)
    met = [lax.ppermute(poles, ("row", "col"), POLES[s]) for s in (0, 1)]
    *coefficients, upper_squares, lower_squares = own_loewner(roots, poles)
    own = own_products(*vectors, *coefficients)

    streams = [(s, batch) for batch in (0, 1) for s in (0, 1)]
    squares = {(s, 1): None for s in (0, 1)} | {(0, 0): upper_squares, (1, 0): lower_squares}
    send, keep, arrived = {}, {}, {}
    *parts, squares[0, 0], squares[1, 0] = partner_loewner(roots, *met, squares[0, 0], squares[1, 0], own[1])
    send[0, 0], raw[0] = meet(raw[0], own[0], parts[0], squares[0, 0])
    send[1, 0] = meet_direct(raw[1], own[1], parts[1], squares[1, 0])
    for s in (0, 1):
        send[s, 1] = add_own(768, raw[s], own[s], parts[s], name=f"meet_{s}_late")
    for s in (0, 1):
        keep[s, 0] = add_own(0, raw[s], own[s], parts[s], name=f"rest_{s}_0")
    after = send[1, 1]
    for phase in (1, 2):
        for at in streams:
            arrived[at] = exchange(send[at], at[0], phase)
        for at in sorted(streams) if phase == 1 else streams:
            if phase == 1 and at[1]:
                s = at[0]
                keep[at] = add_own(512, raw[s], own[s], parts[s], after, name=f"rest_{s}_1")
            half, name = PART << (3 - phase), "add_{}_{}_{}".format(phase, *at)
            send[at], keep[at], squares[at] = add(half, keep[at], arrived[at], squares[at], after, name)
            after = keep[at]
    for at in streams:
        arrived[at] = exchange(send[at], at[0], 3)
    ready = lax.ppermute(after, ("row", "col"), CORES)
    early = join(0, *(group[s, 0] for group in (keep, arrived, squares) for s in (0, 1)), ready)
    late = join(1, *(group[s, 1] for group in (keep, arrived) for s in (0, 1)), early[1])
    return call(
        finish_kernel,
        jax.ShapeDtypeStruct((ROWS, 2, WIDE), F32),
        early[3],
        exchange(early[0], 0, 4),
        *early[1:3],
        exchange(late[0], 0, 4),
        *late[1:3],
        name="finish",
    )


def solution(mesh):
    return jax.shard_map(
        local,
        mesh=mesh,
        in_specs=(
            P("row", "col"),
            P("row", "col"),
            P(),
            P(None, ("col", "row")),
            P(None, ("col", "row")),
            P(None, ("col", "row")),
        ),
        out_specs=P(("row", "col"), None, None),
        check_vma=False,
    )
```
